32 devices in a mesh: gx: 4 (over z), gy: 8 (over y, x, core).
Axes of the slice: x: 2, y: 2, z: 4, core: 2. Of those that a mesh axis runs over, the one named last changes fastest.
Arguments:
- counts: int32 [32], replicated, may hold values from 1 to 12, as said below
- probes: bfloat16 [96, 4, 128, 512], P(None, 'gx', None, 'gy'), may hold values from -6 to 6
- blocks: bfloat16 [4, 8, 12, 24, 128, 128], P('gx', 'gy'), may hold values from -0.0546875 to 0.0546875
- pattern: int32 [4, 8, 12, 24], P('gx', 'gy'), may hold values from 0 to 107, as said below
- coeffs: float32 [4], replicated, may hold values from 0.2 to 1
Outputs:
- applied: float32 [4, 8, 12, 128, 512], P('gx', 'gy')
The draws below stay inside these ranges and needn't reach their ends.
Inputs may be any that keep to these rules, and one draw needn't show every extreme that they name: `counts`: some domain holds exactly 12 panels in every draw. `pattern`: every entry names a live panel of its neighbourhood (below that domain's count). Slots 0 to 7 have code 4 (the own domain), slot 0 the panel itself taken modulo the own count; the other slots have codes other than 4.
All inputs are finite; a program needn't handle non-finite values.
Results may differ from the reference program's by a relative error of at most 0.0047.
Values may be sent and summed in bfloat16 or wider, within the bound.
A program may use at most 192 MiB of HBM per device.

```python
import jax
import jax.numpy as jnp
from jax import lax

B = 128
K = 24
KOWN = 8
CAP = 12
W = 512
STEPS = 3
N_GX = 4
N_GY = 8


def panel_counts(key):
    sub_key = jax.random.fold_in(key, 11)
    key_base, key_heavy = jax.random.split(sub_key)
    domain_count = N_GX * N_GY
    base_counts = jax.random.randint(key_base, (domain_count,), 1, 2 * (CAP // 3))
    ordering = jax.random.permutation(key_heavy, domain_count)
    heavy_count = max(1, domain_count // 32)
    is_heavy = jnp.zeros((domain_count,), jnp.int32).at[ordering[:heavy_count]].set(1)
    result = jnp.where(is_heavy > 0, CAP, base_counts).astype(jnp.int32)
    return (result, ordering[0])


def draw_counts(key, part):
    return panel_counts(key)[0]


def draw_pattern(key, part):
    counts, heavy_first = panel_counts(key)
    key_code, key_pick = jax.random.split(jax.random.fold_in(key, 23))
    shape = (N_GX, N_GY, CAP, K)
    grid_i = jnp.broadcast_to(jnp.arange(N_GX, dtype=jnp.int32)[:, None, None, None], shape)
    grid_j = jnp.broadcast_to(jnp.arange(N_GY, dtype=jnp.int32)[None, :, None, None], shape)
    panels = jnp.broadcast_to(jnp.arange(CAP, dtype=jnp.int32)[None, None, :, None], shape)
    slot_ids = jnp.broadcast_to(jnp.arange(K, dtype=jnp.int32)[None, None, None, :], shape)
    remote_code = jax.random.randint(key_code, shape, 0, 8)
    remote_code = remote_code + (remote_code >= 4).astype(jnp.int32)
    neighbour_code = jnp.where(slot_ids < KOWN, 4, remote_code)
    near_i = (grid_i + neighbour_code // 3 - 1) % N_GX
    near_j = (grid_j + neighbour_code % 3 - 1) % N_GY
    near_count = counts[near_i * N_GY + near_j]
    chosen = jax.random.randint(key_pick, shape, 0, 1 << 20) % near_count
    chosen = jnp.where(slot_ids == 0, panels % near_count, chosen)
    heavy_i = heavy_first // N_GY
    heavy_j = heavy_first % N_GY
    forced = (grid_i == (heavy_i - 1) % N_GX) & (grid_j == (heavy_j - 1) % N_GY) & (panels == 0) & (slot_ids == K - 1)
    neighbour_code = jnp.where(forced, 8, neighbour_code)
    chosen = jnp.where(forced, CAP - 1, chosen)
    return (neighbour_code * CAP + chosen).astype(jnp.int32)


def steps_of(own_key, dims, cuts, smallest, largest):
    gain, own = 1.0, jax.random.fold_in(own_key, 6)
    for position, blocks in cuts:
        steps = jnp.exp(jax.random.uniform(jax.random.fold_in(own, position), (blocks,), jnp.float32, smallest / len(cuts), largest / len(cuts)))
        gain = gain * jnp.repeat(steps, dims[position] // blocks).reshape([-1 if axis == position else 1 for axis in range(len(dims))])
    return gain


def scatter_about(key, extent, width, reach, cuts=(), held_as=jnp.bfloat16):
    values = jax.random.normal(key, extent, jnp.float32) * width
    if len(cuts) > 0:
        values = steps_of(key, extent, cuts, -0.22, 0.18) * values
    return jnp.clip(values, min=-reach, max=reach).astype(held_as)


def setup_inputs(seed: int = 0) -> dict:
    key_of = jax.random.split(jax.random.key(seed), 6)
    return {
        "counts": draw_counts(jax.random.fold_in(key_of[5], 71), 0),
        "probes": scatter_about(key_of[1], (CAP * N_GY, N_GX, B, W), 1.0, 6.0, ((1, 4), (3, 8))),
        "blocks": scatter_about(key_of[2], (N_GX, N_GY, CAP, K, B, B), (4 * K * B) ** -0.5, 0.0546875, ((0, 4), (1, 8))),
        "pattern": draw_pattern(jax.random.fold_in(key_of[5], 71), 0),
        "coeffs": jnp.clip(jax.random.uniform(key_of[4], (STEPS + 1,), jnp.float32, 0.2, 1.0), 0.2, 1.0),
    }


def reference(counts, probes, blocks, pattern, coeffs):
    domain_count = N_GX * N_GY
    offsets = jnp.cumsum(counts) - counts
    panels = jnp.arange(CAP, dtype=jnp.int32)
    is_live = panels[None, :] < counts[:, None]
    global_panel = jnp.where(is_live, offsets[:, None] + panels[None, :], 0).astype(jnp.int32)
    picked = probes[global_panel // N_GX, global_panel % N_GX]
    start_panels = jnp.where(is_live[:, :, None, None], picked, jnp.zeros((), jnp.bfloat16))
    grid_i = (jnp.arange(domain_count, dtype=jnp.int32) // N_GY)[:, None, None]
    grid_j = (jnp.arange(domain_count, dtype=jnp.int32) % N_GY)[:, None, None]
    flat_pattern = pattern.reshape(domain_count, CAP, K)
    neighbour_code = flat_pattern // CAP
    source_domain = ((grid_i + neighbour_code // 3 - 1) % N_GX) * N_GY + (grid_j + neighbour_code % 3 - 1) % N_GY
    source_panel = (source_domain * CAP + flat_pattern % CAP).astype(jnp.int32)
    flat_blocks = blocks.reshape(domain_count, CAP, K, B, B)
    live_mask = is_live.astype(jnp.float32)

    def operate(block_state):
        all_panels = block_state.reshape(domain_count * CAP, B, W)

        def apply_domain(domain_args):
            row_blocks, row_source, row_mask = domain_args
            pieces = all_panels[row_source].astype(jnp.float32)
            summed = jnp.einsum('rkab,rkbw->raw', row_blocks.astype(jnp.float32), pieces)
            return summed * row_mask[:, None, None]

        return lax.map(apply_domain, (flat_blocks, source_panel, live_mask))

    previous = start_panels.astype(jnp.float32)
    current = operate(start_panels)
    result = coeffs[0] * previous + coeffs[1] * current
    for degree in range(2, STEPS + 1):
        sent_panels = current.astype(jnp.bfloat16)
        following = 2.0 * operate(sent_panels) - previous
        result = result + coeffs[degree] * following
        previous, current = current, following
    return result.reshape(N_GX, N_GY, CAP, B, W)
```

```python
import functools

import jax
import jax.numpy as jnp
from jax import lax
from jax.experimental import pallas as pl
from jax.experimental.pallas import tpu as pltpu
from jax.sharding import PartitionSpec as P

OWN = 4
BASE = 7


def pack_kernel(first_ref, held_ref, out_ref, sem):
    slots = held_ref.shape[0]
    domains, per_peer = out_ref.shape[:2]
    for d in range(domains):
        for t in range(per_peer):
            slot = jnp.minimum(first_ref[d] + t, slots - 1)
            pltpu.make_async_copy(held_ref.at[slot], out_ref.at[d, t], sem).start()
    pltpu.make_async_copy(out_ref, out_ref, sem).wait()


def pack(first_slot, held, per_peer):
    return pl.pallas_call(
        pack_kernel,
        out_shape=jax.ShapeDtypeStruct((first_slot.shape[0], per_peer) + held.shape[1:], held.dtype),
        grid_spec=pltpu.PrefetchScalarGridSpec(
            num_scalar_prefetch=1,
            grid=(1,),
            in_specs=[pl.BlockSpec(memory_space=pl.ANY)],
            out_specs=pl.BlockSpec(memory_space=pl.ANY),
            scratch_shapes=[pltpu.SemaphoreType.DMA],
        ),
        name="pack",
    )(first_slot, held)


def step_kernel(mode, base, extras, meta_ref, pattern_ref, coeffs_ref, *refs):
    pieces, refs = refs[:9], refs[9:]
    overflow, refs = refs[:extras], refs[extras:]
    blocks_ref, refs = refs[0], refs[1:]
    halo, acc, sems = refs[-3:]
    refs = refs[:-3]
    r = pl.program_id(0)
    count = meta_ref[0]
    capacity, slots = pattern_ref.shape

    def piece_copy(c):
        size = pieces[c].shape[0]
        return pltpu.make_async_copy(pieces[c], halo.at[pl.ds(c * capacity, size)], sems.at[c])

    def extra_copy(h):
        code = meta_ref[1 + h]
        return pltpu.make_async_copy(
            overflow[h], halo.at[pl.ds(code * capacity + base, capacity - base)], sems.at[9 + h]
        )

    @pl.when(r == 0)
    def _():
        for c in range(9):
            piece_copy(c).start()
        for h in range(extras):
            pl.when(meta_ref[1 + h] >= 0)(lambda h=h: extra_copy(h).start())
        for c in range(9):
            piece_copy(c).wait()
        for h in range(extras):
            pl.when(meta_ref[1 + h] >= 0)(lambda h=h: extra_copy(h).wait())

    @pl.when(r < count)
    def _():
        for k in range(0, slots, 2):
            lhs = jnp.concatenate([blocks_ref[0, k], blocks_ref[0, k + 1]], axis=1)
            rhs = jnp.concatenate([halo[pattern_ref[r, k]], halo[pattern_ref[r, k + 1]]], axis=0)
            part = jnp.dot(lhs, rhs, preferred_element_type=jnp.float32)
            if k == 0:
                acc[...] = part
            else:
                acc[...] += part
        total = acc[...]
        if mode == 1:
            sent_ref, cheb_ref = refs
            cheb_ref[0] = total
            sent_ref[0] = total.astype(sent_ref.dtype)
        elif mode == 2:
            start_ref, sent_ref, cheb_ref = refs
            cheb = 2.0 * total - start_ref[0].astype(jnp.float32)
            cheb_ref[0] = cheb
            sent_ref[0] = cheb.astype(sent_ref.dtype)
        else:
            start_ref, one_ref, two_ref, out_ref = refs
            one = one_ref[0]
            out_ref[0] = (
                coeffs_ref[0] * start_ref[0].astype(jnp.float32)
                + coeffs_ref[1] * one
                + coeffs_ref[2] * two_ref[0]
                + coeffs_ref[3] * (2.0 * total - one)
            )

    @pl.when(r >= count)
    def _():
        for ref in refs if mode == 1 else refs[1:] if mode == 2 else refs[3:]:
            ref[...] = jnp.zeros_like(ref)


def step(mode, base, meta, pattern, coeffs, pieces, overflow, blocks, panels):
    capacity, slots = pattern.shape
    rows, cols = pieces[0].shape[1:]

    def live(r, meta, pattern):
        return jnp.minimum(r, meta[0] - 1)

    panel_in = pl.BlockSpec((1, rows, cols), lambda r, m, p: (live(r, m, p), 0, 0))
    panel_out = pl.BlockSpec((1, rows, cols), lambda r, m, p: (r, 0, 0))
    shape = (capacity, rows, cols)
    wide = jax.ShapeDtypeStruct(shape, jnp.float32)
    narrow = jax.ShapeDtypeStruct(shape, jnp.bfloat16)
    outs = [wide] if mode == 3 else [narrow, wide]
    return pl.pallas_call(
        functools.partial(step_kernel, mode, base, len(overflow)),
        out_shape=outs,
        grid_spec=pltpu.PrefetchScalarGridSpec(
            num_scalar_prefetch=2,
            grid=(capacity,),
            in_specs=[pl.BlockSpec(memory_space=pltpu.SMEM)]
            + [pl.BlockSpec(memory_space=pl.ANY)] * (9 + len(overflow))
            + [pl.BlockSpec((1, slots, rows, rows), lambda r, m, p: (live(r, m, p), 0, 0, 0))]
            + [panel_in] * len(panels),
            out_specs=[panel_out] * len(outs),
            scratch_shapes=[
                pltpu.VMEM((9 * capacity, rows, cols), jnp.bfloat16),
                pltpu.VMEM((rows, cols), jnp.float32),
                pltpu.SemaphoreType.DMA((9 + len(overflow),)),
            ],
        ),
        compiler_params=pltpu.CompilerParams(vmem_limit_bytes=40 * 1024 * 1024),
        name=f"step{mode}",
    )(meta, pattern, coeffs, *pieces, *overflow, blocks, *panels)


def shifted(x, axis, by):
    count = lax.axis_size(axis)
    return lax.ppermute(x, axis, [(i, (i + by) % count) for i in range(count)])


def halo_pieces(panels, base):
    own = panels[:base]
    above, below = shifted(own, "gx", 1), shifted(own, "gx", -1)
    left, right = shifted(own, "gy", 1), shifted(own, "gy", -1)
    return [
        shifted(above, "gy", 1), above, shifted(above, "gy", -1),
        left, panels, right,
        shifted(below, "gy", 1), below, shifted(below, "gy", -1),
    ]


def local(counts, probes, blocks, pattern, coeffs):
    grid_rows = lax.axis_size("gx")
    grid_cols = lax.axis_size("gy")
    domains = grid_rows * grid_cols
    capacity = blocks.shape[2]
    panel_rows = blocks.shape[4]
    probe_cols = probes.shape[3] * grid_cols
    per_peer = (capacity + grid_rows - 1) // grid_rows
    my_row, my_col = lax.axis_index("gx"), lax.axis_index("gy")
    my_domain = my_row * grid_cols + my_col
    ids = jnp.arange(domains, dtype=jnp.int32)
    offsets = jnp.sum(jnp.where(ids[None, :] < ids[:, None], counts[None, :], 0), axis=1)
    my_count = jnp.sum(jnp.where(ids == my_domain, counts, 0))
    my_offset = jnp.sum(jnp.where(ids < my_domain, counts, 0))
    first_slot = (offsets + (my_row - offsets) % grid_rows) // grid_rows
    outgoing = pack(first_slot, probes[:, 0], per_peer)
    arrived = lax.all_to_all(outgoing, ("gx", "gy"), split_axis=0, concat_axis=3, tiled=True)
    arrived = arrived.reshape(per_peer, panel_rows, grid_rows, probe_cols).transpose(0, 2, 1, 3)
    arrived = jnp.concatenate([arrived, arrived], axis=1)
    start = lax.dynamic_slice_in_dim(arrived, my_offset % grid_rows, grid_rows, axis=1)
    start = start.reshape(per_peer * grid_rows, panel_rows, probe_cols)[:capacity]
    rows, table = blocks[0, 0], pattern[0, 0]

    def expand(base, heavy, start):
        meta = [my_count]
        for d in heavy:
            di = (d // grid_cols - my_row + 1) % grid_rows
            dj = (d % grid_cols - my_col + 1) % grid_cols
            near = (d >= 0) & (di < 3) & (dj < 3) & (d != my_domain)
            meta.append(jnp.where(near, di * 3 + dj, -1))
        meta = jnp.stack(meta).astype(jnp.int32)

        def run(mode, panels, *rest):
            overflow = [
                lax.psum(
                    jnp.where(d == my_domain, panels[base:], jnp.zeros((), panels.dtype)), ("gx", "gy")
                )
                for d in heavy
            ]
            pieces = halo_pieces(panels, base)
            return step(mode, base, meta, table, coeffs, pieces, overflow, rows, rest)

        sent, one = run(1, start)
        sent, two = run(2, sent, start)
        (out,) = run(3, sent, start, one, two)
        return out

    base = min(BASE, capacity)
    extras = max(1, domains // 32)
    over = counts > base
    rank = jnp.sum(jnp.where(ids[None, :] < ids[:, None], over[None, :], False), axis=1)
    heavy = [jnp.max(jnp.where(over & (rank == h), ids, -1)) for h in range(extras)]
    out = lax.cond(
        jnp.sum(over) <= extras,
        lambda s: expand(base, heavy, s),
        lambda s: expand(capacity, [], s),
        start,
    )
    return out[None, None]


def solution(mesh):
    in_specs = (
        P(),
        P(None, "gx", None, "gy"),
        P("gx", "gy", None, None, None, None),
        P("gx", "gy", None, None),
        P(),
    )
    out_specs = P("gx", "gy", None, None, None)
    return jax.shard_map(local, mesh=mesh, in_specs=in_specs, out_specs=out_specs, check_vma=False)
```

```python
import functools

import jax
import jax.numpy as jnp
from jax import lax
from jax.experimental import pallas as pl
from jax.experimental.pallas import tpu as pltpu
from jax.sharding import PartitionSpec as P

OWN = 4
BASE = 7


def pack_kernel(first_ref, held_ref, out_ref):
    slots = held_ref.shape[0]
    domains, per_peer = out_ref.shape[:2]

    def one(d, carry):
        for t in range(per_peer):
            out_ref[d, t] = held_ref[jnp.minimum(first_ref[d] + t, slots - 1)]
        return carry

    lax.fori_loop(0, domains, one, 0)


def pack(first_slot, held, per_peer):
    return pl.pallas_call(
        pack_kernel,
        out_shape=jax.ShapeDtypeStruct((first_slot.shape[0], per_peer) + held.shape[1:], held.dtype),
        in_specs=[pl.BlockSpec(memory_space=pltpu.SMEM), pl.BlockSpec(memory_space=pltpu.VMEM)],
        out_specs=pl.BlockSpec(memory_space=pltpu.VMEM),
        compiler_params=pltpu.CompilerParams(vmem_limit_bytes=24 * 1024 * 1024),
        name="pack",
    )(first_slot, held)


def step_kernel(mode, base, extras, meta_ref, pattern_ref, coeffs_ref, *refs):
    pieces, refs = refs[:9], refs[9:]
    overflow, refs = refs[: 3 * extras], refs[3 * extras :]
    blocks_ref, refs = refs[0], refs[1:]
    halo, acc, sems = refs[-3:]
    refs = refs[:-3]
    r = pl.program_id(0)
    count = meta_ref[0]
    capacity, slots = pattern_ref.shape

    def piece_copy(c):
        size = pieces[c].shape[0]
        return pltpu.make_async_copy(pieces[c], halo.at[pl.ds(c * capacity, size)], sems.at[c])

    def extra_copy(h, column):
        code = meta_ref[1 + h]
        return pltpu.make_async_copy(
            overflow[3 * h + column],
            halo.at[pl.ds(code * capacity + base, capacity - base)],
            sems.at[9 + h],
        )

    def each_extra(act):
        for h in range(extras):
            for column in range(3):
                code = meta_ref[1 + h]
                pl.when((code >= 0) & (lax.rem(code, 3) == column))(
                    lambda h=h, column=column: act(extra_copy(h, column))
                )

    @pl.when(r == 0)
    def _():
        for c in range(9):
            piece_copy(c).start()
        each_extra(lambda copy: copy.start())
        for c in range(9):
            piece_copy(c).wait()
        each_extra(lambda copy: copy.wait())

    @pl.when(r < count)
    def _():
        for k in range(0, slots, 2):
            lhs = jnp.concatenate([blocks_ref[0, k], blocks_ref[0, k + 1]], axis=1)
            rhs = jnp.concatenate([halo[pattern_ref[r, k]], halo[pattern_ref[r, k + 1]]], axis=0)
            part = jnp.dot(lhs, rhs, preferred_element_type=jnp.float32)
            if k == 0:
                acc[...] = part
            else:
                acc[...] += part
        total = acc[...]
        if mode == 1:
            sent_ref, cheb_ref = refs
            cheb_ref[0] = total
            sent_ref[0] = total.astype(sent_ref.dtype)
        elif mode == 2:
            start_ref, sent_ref, cheb_ref = refs
            cheb = 2.0 * total - start_ref[0].astype(jnp.float32)
            cheb_ref[0] = cheb
            sent_ref[0] = cheb.astype(sent_ref.dtype)
        else:
            start_ref, one_ref, two_ref, out_ref = refs
            one = one_ref[0]
            out_ref[0] = (
                coeffs_ref[0] * start_ref[0].astype(jnp.float32)
                + coeffs_ref[1] * one
                + coeffs_ref[2] * two_ref[0]
                + coeffs_ref[3] * (2.0 * total - one)
            )

    @pl.when(r >= count)
    def _():
        for ref in refs if mode == 1 else refs[1:] if mode == 2 else refs[3:]:
            ref[...] = jnp.zeros_like(ref)


def step(mode, base, meta, pattern, coeffs, pieces, overflow, blocks, panels):
    capacity, slots = pattern.shape
    rows, cols = pieces[0].shape[1:]

    def live(r, meta, pattern):
        return jnp.minimum(r, meta[0] - 1)

    panel_in = pl.BlockSpec((1, rows, cols), lambda r, m, p: (live(r, m, p), 0, 0))
    panel_out = pl.BlockSpec((1, rows, cols), lambda r, m, p: (r, 0, 0))
    shape = (capacity, rows, cols)
    wide = jax.ShapeDtypeStruct(shape, jnp.float32)
    narrow = jax.ShapeDtypeStruct(shape, jnp.bfloat16)
    outs = [wide] if mode == 3 else [narrow, wide]
    return pl.pallas_call(
        functools.partial(step_kernel, mode, base, len(overflow) // 3),
        out_shape=outs,
        grid_spec=pltpu.PrefetchScalarGridSpec(
            num_scalar_prefetch=2,
            grid=(capacity,),
            in_specs=[pl.BlockSpec(memory_space=pltpu.SMEM)]
            + [pl.BlockSpec(memory_space=pl.ANY)] * (9 + len(overflow))
            + [pl.BlockSpec((1, slots, rows, rows), lambda r, m, p: (live(r, m, p), 0, 0, 0))]
            + [panel_in] * len(panels),
            out_specs=[panel_out] * len(outs),
            scratch_shapes=[
                pltpu.VMEM((9 * capacity, rows, cols), jnp.bfloat16),
                pltpu.VMEM((rows, cols), jnp.float32),
                pltpu.SemaphoreType.DMA((9 + len(overflow),)),
            ],
        ),
        compiler_params=pltpu.CompilerParams(vmem_limit_bytes=40 * 1024 * 1024),
        name=f"step{mode}",
    )(meta, pattern, coeffs, *pieces, *overflow, blocks, *panels)


def shifted(x, axis, by):
    count = lax.axis_size(axis)
    return lax.ppermute(x, axis, [(i, (i + by) % count) for i in range(count)])


def halo_pieces(panels, base):
    own = panels[:base]
    above, below = shifted(own, "gx", 1), shifted(own, "gx", -1)
    left, right = shifted(own, "gy", 1), shifted(own, "gy", -1)
    return [
        shifted(above, "gy", 1), above, shifted(above, "gy", -1),
        left, panels, right,
        shifted(below, "gy", 1), below, shifted(below, "gy", -1),
    ]


def local(counts, probes, blocks, pattern, coeffs):
    grid_rows = lax.axis_size("gx")
    grid_cols = lax.axis_size("gy")
    domains = grid_rows * grid_cols
    capacity = blocks.shape[2]
    panel_rows = blocks.shape[4]
    probe_cols = probes.shape[3] * grid_cols
    per_peer = (capacity + grid_rows - 1) // grid_rows
    my_row, my_col = lax.axis_index("gx"), lax.axis_index("gy")
    my_domain = my_row * grid_cols + my_col
    ids = jnp.arange(domains, dtype=jnp.int32)
    offsets = jnp.sum(jnp.where(ids[None, :] < ids[:, None], counts[None, :], 0), axis=1)
    my_count = jnp.sum(jnp.where(ids == my_domain, counts, 0))
    my_offset = jnp.sum(jnp.where(ids < my_domain, counts, 0))
    first_slot = (offsets + (my_row - offsets) % grid_rows) // grid_rows
    outgoing = pack(first_slot, probes[:, 0], per_peer)
    arrived = lax.all_to_all(outgoing, ("gx", "gy"), split_axis=0, concat_axis=3, tiled=True)
    arrived = arrived.reshape(per_peer, panel_rows, grid_rows, probe_cols).transpose(0, 2, 1, 3)
    arrived = jnp.concatenate([arrived, arrived], axis=1)
    start = lax.dynamic_slice_in_dim(arrived, my_offset % grid_rows, grid_rows, axis=1)
    start = start.reshape(per_peer * grid_rows, panel_rows, probe_cols)[:capacity]
    rows, table = blocks[0, 0], pattern[0, 0]

    def expand(base, heavy, start):
        meta = [my_count]
        for d in heavy:
            di = (d // grid_cols - my_row + 1) % grid_rows
            dj = (d % grid_cols - my_col + 1) % grid_cols
            near = (d >= 0) & (di < 3) & (dj < 3) & (d != my_domain)
            meta.append(jnp.where(near, di * 3 + dj, -1))
        meta = jnp.stack(meta).astype(jnp.int32)

        def run(mode, panels, *rest):
            pieces = halo_pieces(panels, base)
            overflow = []
            if heavy:
                own = panels[base:]
                above, below = shifted(own, "gx", 1), shifted(own, "gx", -1)
            for d in heavy:
                row = (d // grid_cols - my_row + 1) % grid_rows
                middle = jnp.where(row == 0, above, jnp.where(row == 1, own, below))
                overflow += [shifted(middle, "gy", 1), middle, shifted(middle, "gy", -1)]
            return step(mode, base, meta, table, coeffs, pieces, overflow, rows, rest)

        sent, one = run(1, start)
        sent, two = run(2, sent, start)
        (out,) = run(3, sent, start, one, two)
        return out

    base = min(BASE, capacity)
    extras = max(1, domains // 32)
    over = counts > base
    rank = jnp.sum(jnp.where(ids[None, :] < ids[:, None], over[None, :], False), axis=1)
    heavy = [jnp.max(jnp.where(over & (rank == h), ids, -1)) for h in range(extras)]
    out = lax.cond(
        jnp.sum(over) <= extras,
        lambda s: expand(base, heavy, s),
        lambda s: expand(capacity, [], s),
        start,
    )
    return out[None, None]


def solution(mesh):
    in_specs = (
        P(),
        P(None, "gx", None, "gy"),
        P("gx", "gy", None, None, None, None),
        P("gx", "gy", None, None),
        P(),
    )
    out_specs = P("gx", "gy", None, None, None)
    return jax.shard_map(local, mesh=mesh, in_specs=in_specs, out_specs=out_specs, check_vma=False)
```

```python
import functools

import jax
import jax.numpy as jnp
from jax import lax
from jax.experimental import pallas as pl
from jax.experimental.pallas import tpu as pltpu
from jax.sharding import PartitionSpec as P

OWN = 4
BASE = 7


def pack_kernel(first_ref, held_ref, out_ref):
    slots = held_ref.shape[0]
    domains, per_peer = out_ref.shape[:2]

    def one(d, carry):
        for t in range(per_peer):
            out_ref[d, t] = held_ref[jnp.minimum(first_ref[d] + t, slots - 1)]
        return carry

    lax.fori_loop(0, domains, one, 0)


def pack(first_slot, held, per_peer):
    return pl.pallas_call(
        pack_kernel,
        out_shape=jax.ShapeDtypeStruct((first_slot.shape[0], per_peer) + held.shape[1:], held.dtype),
        in_specs=[pl.BlockSpec(memory_space=pltpu.SMEM), pl.BlockSpec(memory_space=pltpu.VMEM)],
        out_specs=pl.BlockSpec(memory_space=pltpu.VMEM),
        compiler_params=pltpu.CompilerParams(vmem_limit_bytes=24 * 1024 * 1024),
        name="pack",
    )(first_slot, held)


def step_kernel(mode, base, extras, meta_ref, pattern_ref, coeffs_ref, *refs):
    panels_ref, ring_ref, refs = refs[0], refs[1], refs[2:]
    if extras:
        extra_ref, refs = refs[0], refs[1:]
    blocks_ref, refs = refs[0], refs[1:]
    halo, acc, sems = refs[-3:]
    refs = refs[:-3]
    r = pl.program_id(0)
    count = meta_ref[0]
    capacity, slots = pattern_ref.shape

    def piece_copy(c):
        source = panels_ref if c == OWN else ring_ref.at[c]
        return pltpu.make_async_copy(
            source, halo.at[pl.ds(c * capacity, source.shape[0])], sems.at[c]
        )

    def extra_copy(h, column):
        code = meta_ref[1 + h]
        return pltpu.make_async_copy(
            extra_ref.at[h, column],
            halo.at[pl.ds(code * capacity + base, capacity - base)],
            sems.at[9 + h],
        )

    def each_extra(act):
        for h in range(extras):
            for column in range(3):
                code = meta_ref[1 + h]
                pl.when((code >= 0) & (lax.rem(code, 3) == column))(
                    lambda h=h, column=column: act(extra_copy(h, column))
                )

    @pl.when(r == 0)
    def _():
        for c in range(9):
            piece_copy(c).start()
        each_extra(lambda copy: copy.start())
        for c in range(9):
            piece_copy(c).wait()
        each_extra(lambda copy: copy.wait())

    @pl.when(r < count)
    def _():
        for k in range(0, slots, 2):
            lhs = jnp.concatenate([blocks_ref[0, k], blocks_ref[0, k + 1]], axis=1)
            rhs = jnp.concatenate([halo[pattern_ref[r, k]], halo[pattern_ref[r, k + 1]]], axis=0)
            part = jnp.dot(lhs, rhs, preferred_element_type=jnp.float32)
            if k == 0:
                acc[...] = part
            else:
                acc[...] += part
        total = acc[...]
        if mode == 1:
            sent_ref, cheb_ref = refs
            cheb_ref[0] = total
            sent_ref[0] = total.astype(sent_ref.dtype)
        elif mode == 2:
            start_ref, sent_ref, cheb_ref = refs
            cheb = 2.0 * total - start_ref[0].astype(jnp.float32)
            cheb_ref[0] = cheb
            sent_ref[0] = cheb.astype(sent_ref.dtype)
        else:
            start_ref, one_ref, two_ref, out_ref = refs
            one = one_ref[0]
            out_ref[0] = (
                coeffs_ref[0] * start_ref[0].astype(jnp.float32)
                + coeffs_ref[1] * one
                + coeffs_ref[2] * two_ref[0]
                + coeffs_ref[3] * (2.0 * total - one)
            )

    @pl.when(r >= count)
    def _():
        for ref in refs if mode == 1 else refs[1:] if mode == 2 else refs[3:]:
            ref[...] = jnp.zeros_like(ref)


def step(mode, base, meta, pattern, coeffs, pieces, blocks, panels):
    capacity, slots = pattern.shape
    rows, cols = pieces[0].shape[1:]
    extras = meta.shape[0] - 1

    def live(r, meta, pattern):
        return jnp.minimum(r, meta[0] - 1)

    panel_in = pl.BlockSpec((1, rows, cols), lambda r, m, p: (live(r, m, p), 0, 0))
    panel_out = pl.BlockSpec((1, rows, cols), lambda r, m, p: (r, 0, 0))
    shape = (capacity, rows, cols)
    wide = jax.ShapeDtypeStruct(shape, jnp.float32)
    narrow = jax.ShapeDtypeStruct(shape, jnp.bfloat16)
    outs = [wide] if mode == 3 else [narrow, wide]
    return pl.pallas_call(
        functools.partial(step_kernel, mode, base, extras),
        out_shape=outs,
        grid_spec=pltpu.PrefetchScalarGridSpec(
            num_scalar_prefetch=2,
            grid=(capacity,),
            in_specs=[pl.BlockSpec(memory_space=pltpu.SMEM)]
            + [pl.BlockSpec(memory_space=pl.ANY)] * len(pieces)
            + [pl.BlockSpec((1, slots, rows, rows), lambda r, m, p: (live(r, m, p), 0, 0, 0))]
            + [panel_in] * len(panels),
            out_specs=[panel_out] * len(outs),
            scratch_shapes=[
                pltpu.VMEM((9 * capacity, rows, cols), jnp.bfloat16),
                pltpu.VMEM((rows, cols), jnp.float32),
                pltpu.SemaphoreType.DMA((9 + extras,)),
            ],
        ),
        compiler_params=pltpu.CompilerParams(vmem_limit_bytes=40 * 1024 * 1024),
        name=f"step{mode}",
    )(meta, pattern, coeffs, *pieces, blocks, *panels)


def halo_kernel(base, tails, extras, heavy_ref, panels_ref, *refs):
    halo_ref, refs = refs[0], refs[1:]
    if extras:
        extra_ref, near, own, middle, local_sem, extra_sems, keep_sem = refs[:7]
        refs = refs[7:]
    z_sems, row_sems, corner_sems = refs
    row, col = lax.axis_index("gx"), lax.axis_index("gy")
    rows, cols = lax.axis_size("gx"), lax.axis_size("gy")
    vertical = ((lax.rem(row + 1, rows), col), (lax.rem(row + rows - 1, rows), col))
    sideways = ((row, lax.rem(col + 1, cols)), (row, lax.rem(col + cols - 1, cols)))
    barrier = pltpu.get_barrier_semaphore()
    for target in vertical + sideways:
        pl.semaphore_signal(barrier, inc=1, device_id=target, device_id_type=pl.DeviceIdType.MESH)
    pl.semaphore_wait(barrier, 4)

    def remote(src, dst, sems, target):
        return pltpu.make_async_remote_copy(
            src_ref=src,
            dst_ref=dst,
            send_sem=sems.at[0],
            recv_sem=sems.at[1],
            device_id=target,
            device_id_type=pl.DeviceIdType.MESH,
        )

    half = (base + 1) // 2
    chunks = [(0, half), (half, base - half)]
    if extras:
        for start, size in tails:
            chunks.append((start, size))
    z_copies, others = [], []
    for n, (start, size) in enumerate(chunks):
        pair = []
        for v in range(2):
            if start < base:
                dst = halo_ref.at[6 * v + 1, pl.ds(start, size)]
            else:
                dst = near.at[v, pl.ds(start - base, size)]
            pair.append(remote(panels_ref.at[pl.ds(start, size)], dst, z_sems.at[n, v], vertical[v]))
        z_copies.append(pair)

    def begin(copies):
        for copy in copies:
            copy.start()

    begin(z_copies[0])
    row_copies = [
        remote(panels_ref.at[pl.ds(0, base)], halo_ref.at[3 + 2 * h], row_sems.at[h], sideways[h])
        for h in range(2)
    ]
    begin(row_copies)
    others += row_copies
    begin(z_copies[1])
    if extras:
        mine = pltpu.make_async_copy(panels_ref.at[pl.ds(base, own.shape[0])], own, local_sem)
        mine.start()
        mine.wait()
    for n, (start, size) in enumerate(chunks):
        for copy in z_copies[n]:
            copy.wait_recv()
        if n + 2 < len(chunks):
            begin(z_copies[n + 2])
        if start < base:
            for v in range(2):
                part = pl.ds(start, size)
                copies = [
                    remote(
                        halo_ref.at[6 * v + 1, part],
                        halo_ref.at[6 * v + 2 * h, part],
                        corner_sems.at[n, v, h],
                        sideways[h],
                    )
                    for h in range(2)
                ]
                begin(copies)
                others += copies
        else:
            for e in range(extras):
                away = heavy_ref[e]
                for p in range(start - base, start - base + size):
                    middle[e, p] = jnp.where(
                        away == 0, near[0, p], jnp.where(away == 1, own[p], near[1, p])
                    )
                part = pl.ds(start - base, size)
                copies = [
                    remote(
                        middle.at[e, part],
                        extra_ref.at[e, 2 * h, part],
                        extra_sems.at[n - 2, e, h],
                        sideways[h],
                    )
                    for h in range(2)
                ]
                begin(copies)
                others += copies
    if extras:
        kept = [
            pltpu.make_async_copy(middle.at[e], extra_ref.at[e, 1], keep_sem.at[e]) for e in range(extras)
        ]
        begin(kept)
        for copy in kept:
            copy.wait()
    for pair in z_copies:
        for copy in pair:
            copy.wait_send()
    for copy in others:
        copy.wait()


def halo(panels, base, heavy_rows):
    capacity, rows, cols = panels.shape
    extras, rest = len(heavy_rows), capacity - base
    dma = pltpu.SemaphoreType.DMA
    outs = [jax.ShapeDtypeStruct((9, base, rows, cols), panels.dtype)]
    scratch, tails = [], []
    if extras:
        half = (rest + 1) // 2
        tails = [(base, half), (base + half, rest - half)]
        outs.append(jax.ShapeDtypeStruct((extras, 3, rest, rows, cols), panels.dtype))
        scratch = [
            pltpu.VMEM((2, rest, rows, cols), panels.dtype),
            pltpu.VMEM((rest, rows, cols), panels.dtype),
            pltpu.VMEM((extras, rest, rows, cols), panels.dtype),
            dma,
            dma((2, extras, 2, 2)),
            dma((extras,)),
        ]
    scratch += [dma((4, 2, 2)), dma((2, 2)), dma((2, 2, 2, 2))]
    away = jnp.stack(heavy_rows) if extras else jnp.zeros((1,), jnp.int32)
    return pl.pallas_call(
        functools.partial(halo_kernel, base, tails, extras),
        out_shape=outs,
        in_specs=[pl.BlockSpec(memory_space=pltpu.SMEM), pl.BlockSpec(memory_space=pl.ANY)],
        out_specs=[pl.BlockSpec(memory_space=pl.ANY)] * len(outs),
        scratch_shapes=scratch,
        compiler_params=pltpu.CompilerParams(
            collective_id=0 if extras else 1,
            has_side_effects=True,
            vmem_limit_bytes=32 * 1024 * 1024,
        ),
        name="halo_part" if extras else "halo_full",
    )(away.astype(jnp.int32), panels)


def local(counts, probes, blocks, pattern, coeffs):
    grid_rows = lax.axis_size("gx")
    grid_cols = lax.axis_size("gy")
    domains = grid_rows * grid_cols
    capacity = blocks.shape[2]
    panel_rows = blocks.shape[4]
    probe_cols = probes.shape[3] * grid_cols
    per_peer = (capacity + grid_rows - 1) // grid_rows
    my_row, my_col = lax.axis_index("gx"), lax.axis_index("gy")
    my_domain = my_row * grid_cols + my_col
    ids = jnp.arange(domains, dtype=jnp.int32)
    offsets = jnp.sum(jnp.where(ids[None, :] < ids[:, None], counts[None, :], 0), axis=1)
    my_count = jnp.sum(jnp.where(ids == my_domain, counts, 0))
    my_offset = jnp.sum(jnp.where(ids < my_domain, counts, 0))
    first_slot = (offsets + (my_row - offsets) % grid_rows) // grid_rows
    outgoing = pack(first_slot, probes[:, 0], per_peer)
    arrived = lax.all_to_all(outgoing, ("gx", "gy"), split_axis=0, concat_axis=3, tiled=True)
    arrived = arrived.reshape(per_peer, panel_rows, grid_rows, probe_cols).transpose(0, 2, 1, 3)
    arrived = jnp.concatenate([arrived, arrived], axis=1)
    start = lax.dynamic_slice_in_dim(arrived, my_offset % grid_rows, grid_rows, axis=1)
    start = start.reshape(per_peer * grid_rows, panel_rows, probe_cols)[:capacity]
    rows, table = blocks[0, 0], pattern[0, 0]

    def expand(base, heavy, start):
        meta, heavy_rows = [my_count], []
        for d in heavy:
            di = (d // grid_cols - my_row + 1) % grid_rows
            dj = (d % grid_cols - my_col + 1) % grid_cols
            near = (d >= 0) & (di < 3) & (dj < 3) & (d != my_domain)
            heavy_rows.append(di)
            meta.append(jnp.where(near, di * 3 + dj, -1))
        meta = jnp.stack(meta).astype(jnp.int32)

        def run(mode, panels, *rest):
            ring, *extra = halo(panels, base, heavy_rows)
            return step(mode, base, meta, table, coeffs, [panels, ring] + extra, rows, rest)

        sent, one = run(1, start)
        sent, two = run(2, sent, start)
        (out,) = run(3, sent, start, one, two)
        return out

    base = min(BASE, capacity)
    extras = max(1, domains // 32)
    over = counts > base
    rank = jnp.sum(jnp.where(ids[None, :] < ids[:, None], over[None, :], False), axis=1)
    heavy = [jnp.max(jnp.where(over & (rank == h), ids, -1)) for h in range(extras)]
    out = lax.cond(
        jnp.sum(over) <= extras,
        lambda s: expand(base, heavy, s),
        lambda s: expand(capacity, [], s),
        start,
    )
    return out[None, None]


def solution(mesh):
    in_specs = (
        P(),
        P(None, "gx", None, "gy"),
        P("gx", "gy", None, None, None, None),
        P("gx", "gy", None, None),
        P(),
    )
    out_specs = P("gx", "gy", None, None, None)
    return jax.shard_map(local, mesh=mesh, in_specs=in_specs, out_specs=out_specs, check_vma=False)
```

```python
import functools

import jax
import jax.numpy as jnp
from jax import lax
from jax.experimental import pallas as pl
from jax.experimental.pallas import tpu as pltpu
from jax.sharding import PartitionSpec as P

OWN = 4
BASE = 7


def pack_kernel(first_ref, held_ref, out_ref):
    slots = held_ref.shape[0]
    domains, per_peer = out_ref.shape[:2]

    def one(d, carry):
        for t in range(per_peer):
            out_ref[d, t] = held_ref[jnp.minimum(first_ref[d] + t, slots - 1)]
        return carry

    lax.fori_loop(0, domains, one, 0)


def pack(first_slot, held, per_peer):
    return pl.pallas_call(
        pack_kernel,
        out_shape=jax.ShapeDtypeStruct((first_slot.shape[0], per_peer) + held.shape[1:], held.dtype),
        in_specs=[pl.BlockSpec(memory_space=pltpu.SMEM), pl.BlockSpec(memory_space=pltpu.VMEM)],
        out_specs=pl.BlockSpec(memory_space=pltpu.VMEM),
        compiler_params=pltpu.CompilerParams(vmem_limit_bytes=24 * 1024 * 1024),
        name="pack",
    )(first_slot, held)


def step_kernel(mode, base, extras, meta_ref, pattern_ref, coeffs_ref, *refs):
    panels_ref, ring_ref, refs = refs[0], refs[1], refs[2:]
    if extras:
        extra_ref, refs = refs[0], refs[1:]
    blocks_ref, refs = refs[0], refs[1:]
    halo, acc, sems = refs[-3:]
    refs = refs[:-3]
    r = pl.program_id(0)
    count = meta_ref[0]
    capacity, slots = pattern_ref.shape

    def piece_copy(c):
        source = panels_ref if c == OWN else ring_ref.at[c]
        return pltpu.make_async_copy(
            source, halo.at[pl.ds(c * capacity, source.shape[0])], sems.at[c]
        )

    def extra_copy(h, column):
        code = meta_ref[1 + h]
        return pltpu.make_async_copy(
            extra_ref.at[h, column],
            halo.at[pl.ds(code * capacity + base, capacity - base)],
            sems.at[9 + h],
        )

    def each_extra(act):
        for h in range(extras):
            for column in range(3):
                code = meta_ref[1 + h]
                pl.when((code >= 0) & (lax.rem(code, 3) == column))(
                    lambda h=h, column=column: act(extra_copy(h, column))
                )

    @pl.when(r == 0)
    def _():
        for c in range(9):
            piece_copy(c).start()
        each_extra(lambda copy: copy.start())
        for c in range(9):
            piece_copy(c).wait()
        each_extra(lambda copy: copy.wait())

    @pl.when(r < count)
    def _():
        for k in range(0, slots, 2):
            lhs = jnp.concatenate([blocks_ref[0, k], blocks_ref[0, k + 1]], axis=1)
            rhs = jnp.concatenate([halo[pattern_ref[r, k]], halo[pattern_ref[r, k + 1]]], axis=0)
            part = jnp.dot(lhs, rhs, preferred_element_type=jnp.float32)
            if k == 0:
                acc[...] = part
            else:
                acc[...] += part
        total = acc[...]
        if mode == 1:
            sent_ref, cheb_ref = refs
            cheb_ref[0] = total
            sent_ref[0] = total.astype(sent_ref.dtype)
        elif mode == 2:
            start_ref, sent_ref, cheb_ref = refs
            cheb = 2.0 * total - start_ref[0].astype(jnp.float32)
            cheb_ref[0] = cheb
            sent_ref[0] = cheb.astype(sent_ref.dtype)
        else:
            start_ref, one_ref, two_ref, out_ref = refs
            one = one_ref[0]
            out_ref[0] = (
                coeffs_ref[0] * start_ref[0].astype(jnp.float32)
                + coeffs_ref[1] * one
                + coeffs_ref[2] * two_ref[0]
                + coeffs_ref[3] * (2.0 * total - one)
            )

    @pl.when(r >= count)
    def _():
        for ref in refs if mode == 1 else refs[1:] if mode == 2 else refs[3:]:
            ref[...] = jnp.zeros_like(ref)


def step(mode, base, meta, pattern, coeffs, pieces, blocks, panels):
    capacity, slots = pattern.shape
    rows, cols = pieces[0].shape[1:]
    extras = meta.shape[0] - 1

    def live(r, meta, pattern):
        return jnp.minimum(r, meta[0] - 1)

    panel_in = pl.BlockSpec((1, rows, cols), lambda r, m, p: (live(r, m, p), 0, 0))
    panel_out = pl.BlockSpec((1, rows, cols), lambda r, m, p: (r, 0, 0))
    shape = (capacity, rows, cols)
    wide = jax.ShapeDtypeStruct(shape, jnp.float32)
    narrow = jax.ShapeDtypeStruct(shape, jnp.bfloat16)
    outs = [wide] if mode == 3 else [narrow, wide]
    return pl.pallas_call(
        functools.partial(step_kernel, mode, base, extras),
        out_shape=outs,
        grid_spec=pltpu.PrefetchScalarGridSpec(
            num_scalar_prefetch=2,
            grid=(capacity,),
            in_specs=[pl.BlockSpec(memory_space=pltpu.SMEM)]
            + [pl.BlockSpec(memory_space=pl.ANY)] * len(pieces)
            + [pl.BlockSpec((1, slots, rows, rows), lambda r, m, p: (live(r, m, p), 0, 0, 0))]
            + [panel_in] * len(panels),
            out_specs=[panel_out] * len(outs),
            scratch_shapes=[
                pltpu.VMEM((9 * capacity, rows, cols), jnp.bfloat16),
                pltpu.VMEM((rows, cols), jnp.float32),
                pltpu.SemaphoreType.DMA((9 + extras,)),
            ],
        ),
        compiler_params=pltpu.CompilerParams(vmem_limit_bytes=58 * 1024 * 1024),
        name=f"step{mode}",
    )(meta, pattern, coeffs, *pieces, blocks, *panels)


PARTS = 3
AHEAD = 3


def cut(low, high):
    edges = [low + -((low - high) * n // PARTS) for n in range(PARTS + 1)]
    return [(a, b - a) for a, b in zip(edges, edges[1:]) if b > a]


def halo_kernel(base, extras, heavy_ref, panels_ref, *refs):
    halo_ref, refs = refs[0], refs[1:]
    if extras:
        extra_ref, near, own, middle, local_sem, extra_sems, keep_sem = refs[:7]
        refs = refs[7:]
    z_sems, row_sems, corner_sems = refs
    row, col = lax.axis_index("gx"), lax.axis_index("gy")
    rows, cols = lax.axis_size("gx"), lax.axis_size("gy")
    vertical = ((lax.rem(row + 1, rows), col), (lax.rem(row + rows - 1, rows), col))
    sideways = ((row, lax.rem(col + 1, cols)), (row, lax.rem(col + cols - 1, cols)))
    barrier = pltpu.get_barrier_semaphore()
    for target in vertical + sideways:
        pl.semaphore_signal(barrier, inc=1, device_id=target, device_id_type=pl.DeviceIdType.MESH)
    pl.semaphore_wait(barrier, 4)

    def remote(src, dst, sems, target):
        return pltpu.make_async_remote_copy(
            src_ref=src,
            dst_ref=dst,
            send_sem=sems.at[0],
            recv_sem=sems.at[1],
            device_id=target,
            device_id_type=pl.DeviceIdType.MESH,
        )

    chunks = cut(0, base)
    first_tail = len(chunks)
    if extras:
        chunks += cut(base, panels_ref.shape[0])
    z_copies, others = [], []
    for n, (start, size) in enumerate(chunks):
        pair = []
        for v in range(2):
            if start < base:
                dst = halo_ref.at[6 * v + 1, pl.ds(start, size)]
            else:
                dst = near.at[v, pl.ds(start - base, size)]
            pair.append(remote(panels_ref.at[pl.ds(start, size)], dst, z_sems.at[n, v], vertical[v]))
        z_copies.append(pair)

    def begin(copies):
        for copy in copies:
            copy.start()

    begin(z_copies[0])
    row_copies = [
        remote(panels_ref.at[pl.ds(0, base)], halo_ref.at[3 + 2 * h], row_sems.at[h], sideways[h])
        for h in range(2)
    ]
    begin(row_copies)
    others += row_copies
    for pair in z_copies[1:AHEAD]:
        begin(pair)
    if extras:
        mine = pltpu.make_async_copy(panels_ref.at[pl.ds(base, own.shape[0])], own, local_sem)
        mine.start()
        mine.wait()
    for n, (start, size) in enumerate(chunks):
        for copy in z_copies[n]:
            copy.wait_recv()
        if n + AHEAD < len(chunks):
            begin(z_copies[n + AHEAD])
        if start < base:
            for v in range(2):
                part = pl.ds(start, size)
                copies = [
                    remote(
                        halo_ref.at[6 * v + 1, part],
                        halo_ref.at[6 * v + 2 * h, part],
                        corner_sems.at[n, v, h],
                        sideways[h],
                    )
                    for h in range(2)
                ]
                begin(copies)
                others += copies
        else:
            for e in range(extras):
                away = heavy_ref[e]
                for p in range(start - base, start - base + size):
                    middle[e, p] = jnp.where(
                        away == 0, near[0, p], jnp.where(away == 1, own[p], near[1, p])
                    )
                part = pl.ds(start - base, size)
                copies = [
                    remote(
                        middle.at[e, part],
                        extra_ref.at[e, 2 * h, part],
                        extra_sems.at[n - first_tail, e, h],
                        sideways[h],
                    )
                    for h in range(2)
                ]
                begin(copies)
                others += copies
    if extras:
        kept = [
            pltpu.make_async_copy(middle.at[e], extra_ref.at[e, 1], keep_sem.at[e]) for e in range(extras)
        ]
        begin(kept)
        for copy in kept:
            copy.wait()
    for pair in z_copies:
        for copy in pair:
            copy.wait_send()
    for copy in others:
        copy.wait()


def halo(panels, base, heavy_rows):
    capacity, rows, cols = panels.shape
    extras, rest = len(heavy_rows), capacity - base
    dma = pltpu.SemaphoreType.DMA
    outs = [jax.ShapeDtypeStruct((9, base, rows, cols), panels.dtype)]
    scratch = []
    if extras:
        outs.append(jax.ShapeDtypeStruct((extras, 3, rest, rows, cols), panels.dtype))
        scratch = [
            pltpu.VMEM((2, rest, rows, cols), panels.dtype),
            pltpu.VMEM((rest, rows, cols), panels.dtype),
            pltpu.VMEM((extras, rest, rows, cols), panels.dtype),
            dma,
            dma((PARTS, extras, 2, 2)),
            dma((extras,)),
        ]
    scratch += [dma((2 * PARTS, 2, 2)), dma((2, 2)), dma((PARTS, 2, 2, 2))]
    away = jnp.stack(heavy_rows) if extras else jnp.zeros((1,), jnp.int32)
    return pl.pallas_call(
        functools.partial(halo_kernel, base, extras),
        out_shape=outs,
        in_specs=[pl.BlockSpec(memory_space=pltpu.SMEM), pl.BlockSpec(memory_space=pl.ANY)],
        out_specs=[pl.BlockSpec(memory_space=pl.ANY)] * len(outs),
        scratch_shapes=scratch,
        compiler_params=pltpu.CompilerParams(
            collective_id=0 if extras else 1,
            has_side_effects=True,
            vmem_limit_bytes=58 * 1024 * 1024,
        ),
        name="halo_part" if extras else "halo_full",
    )(away.astype(jnp.int32), panels)


def local(counts, probes, blocks, pattern, coeffs):
    grid_rows = lax.axis_size("gx")
    grid_cols = lax.axis_size("gy")
    domains = grid_rows * grid_cols
    capacity = blocks.shape[2]
    panel_rows = blocks.shape[4]
    probe_cols = probes.shape[3] * grid_cols
    per_peer = (capacity + grid_rows - 1) // grid_rows
    my_row, my_col = lax.axis_index("gx"), lax.axis_index("gy")
    my_domain = my_row * grid_cols + my_col
    ids = jnp.arange(domains, dtype=jnp.int32)
    offsets = jnp.sum(jnp.where(ids[None, :] < ids[:, None], counts[None, :], 0), axis=1)
    my_count = jnp.sum(jnp.where(ids == my_domain, counts, 0))
    my_offset = jnp.sum(jnp.where(ids < my_domain, counts, 0))
    first_slot = (offsets + (my_row - offsets) % grid_rows) // grid_rows
    outgoing = pack(first_slot, probes[:, 0], per_peer)
    arrived = lax.all_to_all(outgoing, ("gx", "gy"), split_axis=0, concat_axis=3, tiled=True)
    arrived = arrived.reshape(per_peer, panel_rows, grid_rows, probe_cols).transpose(0, 2, 1, 3)
    arrived = jnp.concatenate([arrived, arrived], axis=1)
    start = lax.dynamic_slice_in_dim(arrived, my_offset % grid_rows, grid_rows, axis=1)
    start = start.reshape(per_peer * grid_rows, panel_rows, probe_cols)[:capacity]
    rows, table = blocks[0, 0], pattern[0, 0]

    def expand(base, heavy, start):
        meta, heavy_rows = [my_count], []
        for d in heavy:
            di = (d // grid_cols - my_row + 1) % grid_rows
            dj = (d % grid_cols - my_col + 1) % grid_cols
            near = (d >= 0) & (di < 3) & (dj < 3) & (d != my_domain)
            heavy_rows.append(di)
            meta.append(jnp.where(near, di * 3 + dj, -1))
        meta = jnp.stack(meta).astype(jnp.int32)

        def run(mode, panels, *rest):
            ring, *extra = halo(panels, base, heavy_rows)
            return step(mode, base, meta, table, coeffs, [panels, ring] + extra, rows, rest)

        sent, one = run(1, start)
        sent, two = run(2, sent, start)
        (out,) = run(3, sent, start, one, two)
        return out

    base = min(BASE, capacity)
    extras = max(1, domains // 32)
    over = counts > base
    rank = jnp.sum(jnp.where(ids[None, :] < ids[:, None], over[None, :], False), axis=1)
    heavy = [jnp.max(jnp.where(over & (rank == h), ids, -1)) for h in range(extras)]
    out = lax.cond(
        jnp.sum(over) <= extras,
        lambda s: expand(base, heavy, s),
        lambda s: expand(capacity, [], s),
        start,
    )
    return out[None, None]


def solution(mesh):
    in_specs = (
        P(),
        P(None, "gx", None, "gy"),
        P("gx", "gy", None, None, None, None),
        P("gx", "gy", None, None),
        P(),
    )
    out_specs = P("gx", "gy", None, None, None)
    return jax.shard_map(local, mesh=mesh, in_specs=in_specs, out_specs=out_specs, check_vma=False)
```

```python
import functools

import jax
import jax.numpy as jnp
from jax import lax
from jax.experimental import pallas as pl
from jax.experimental.pallas import tpu as pltpu
from jax.sharding import PartitionSpec as P

OWN = 4
BASE = 7


def pack_kernel(first_ref, held_ref, out_ref):
    slots = held_ref.shape[0]
    domains, per_peer = out_ref.shape[:2]

    def one(d, carry):
        for t in range(per_peer):
            out_ref[d, t] = held_ref[jnp.minimum(first_ref[d] + t, slots - 1)]
        return carry

    lax.fori_loop(0, domains, one, 0)


def pack(first_slot, held, per_peer):
    return pl.pallas_call(
        pack_kernel,
        out_shape=jax.ShapeDtypeStruct((first_slot.shape[0], per_peer) + held.shape[1:], held.dtype),
        in_specs=[pl.BlockSpec(memory_space=pltpu.SMEM), pl.BlockSpec(memory_space=pltpu.VMEM)],
        out_specs=pl.BlockSpec(memory_space=pltpu.VMEM),
        compiler_params=pltpu.CompilerParams(vmem_limit_bytes=24 * 1024 * 1024),
        name="pack",
    )(first_slot, held)


def step_kernel(mode, base, extras, meta_ref, pattern_ref, coeffs_ref, *refs):
    panels_ref, ring_ref, refs = refs[0], refs[1], refs[2:]
    if extras:
        extra_ref, refs = refs[0], refs[1:]
    blocks_ref, refs = refs[0], refs[1:]
    halo, acc, sems = refs[-3:]
    refs = refs[:-3]
    r = pl.program_id(0)
    count = meta_ref[0]
    capacity, slots = pattern_ref.shape

    def piece_copy(c):
        source = panels_ref if c == OWN else ring_ref.at[c]
        return pltpu.make_async_copy(
            source, halo.at[pl.ds(c * capacity, source.shape[0])], sems.at[c]
        )

    def extra_copy(h, column):
        code = meta_ref[1 + h]
        return pltpu.make_async_copy(
            extra_ref.at[h, column],
            halo.at[pl.ds(code * capacity + base, capacity - base)],
            sems.at[9 + h],
        )

    def each_extra(act):
        for h in range(extras):
            for column in range(3):
                code = meta_ref[1 + h]
                pl.when((code >= 0) & (lax.rem(code, 3) == column))(
                    lambda h=h, column=column: act(extra_copy(h, column))
                )

    @pl.when(r == 0)
    def _():
        for c in range(9):
            piece_copy(c).start()
        each_extra(lambda copy: copy.start())
        for c in range(9):
            piece_copy(c).wait()
        each_extra(lambda copy: copy.wait())

    @pl.when(r < count)
    def _():
        for k in range(0, slots, 2):
            lhs = jnp.concatenate([blocks_ref[0, k], blocks_ref[0, k + 1]], axis=1)
            rhs = jnp.concatenate([halo[pattern_ref[r, k]], halo[pattern_ref[r, k + 1]]], axis=0)
            part = jnp.dot(lhs, rhs, preferred_element_type=jnp.float32)
            if k == 0:
                acc[...] = part
            else:
                acc[...] += part
        total = acc[...]
        if mode == 1:
            sent_ref, cheb_ref = refs
            cheb_ref[0] = total
            sent_ref[0] = total.astype(sent_ref.dtype)
        elif mode == 2:
            start_ref, sent_ref, cheb_ref = refs
            cheb = 2.0 * total - start_ref[0].astype(jnp.float32)
            cheb_ref[0] = cheb
            sent_ref[0] = cheb.astype(sent_ref.dtype)
        else:
            start_ref, one_ref, two_ref, out_ref = refs
            one = one_ref[0]
            out_ref[0] = (
                coeffs_ref[0] * start_ref[0].astype(jnp.float32)
                + coeffs_ref[1] * one
                + coeffs_ref[2] * two_ref[0]
                + coeffs_ref[3] * (2.0 * total - one)
            )

    @pl.when(r >= count)
    def _():
        for ref in refs if mode == 1 else refs[1:] if mode == 2 else refs[3:]:
            ref[...] = jnp.zeros_like(ref)


def step(mode, base, meta, pattern, coeffs, pieces, blocks, panels):
    capacity, slots = pattern.shape
    rows, cols = pieces[0].shape[1:]
    extras = meta.shape[0] - 1

    def live(r, meta, pattern):
        return jnp.minimum(r, meta[0] - 1)

    panel_in = pl.BlockSpec((1, rows, cols), lambda r, m, p: (live(r, m, p), 0, 0))
    panel_out = pl.BlockSpec((1, rows, cols), lambda r, m, p: (r, 0, 0))
    shape = (capacity, rows, cols)
    wide = jax.ShapeDtypeStruct(shape, jnp.float32)
    narrow = jax.ShapeDtypeStruct(shape, jnp.bfloat16)
    outs = [wide] if mode == 3 else [narrow, wide]
    return pl.pallas_call(
        functools.partial(step_kernel, mode, base, extras),
        out_shape=outs,
        grid_spec=pltpu.PrefetchScalarGridSpec(
            num_scalar_prefetch=2,
            grid=(capacity,),
            in_specs=[pl.BlockSpec(memory_space=pltpu.SMEM)]
            + [pl.BlockSpec(memory_space=pl.ANY)] * len(pieces)
            + [pl.BlockSpec((1, slots, rows, rows), lambda r, m, p: (live(r, m, p), 0, 0, 0))]
            + [panel_in] * len(panels),
            out_specs=[panel_out] * len(outs),
            scratch_shapes=[
                pltpu.VMEM((9 * capacity, rows, cols), jnp.bfloat16),
                pltpu.VMEM((rows, cols), jnp.float32),
                pltpu.SemaphoreType.DMA((9 + extras,)),
            ],
        ),
        compiler_params=pltpu.CompilerParams(vmem_limit_bytes=58 * 1024 * 1024),
        name=f"step{mode}",
    )(meta, pattern, coeffs, *pieces, blocks, *panels)


PARTS = 3
AHEAD = 3


def cut(low, high):
    edges = [low + -((low - high) * n // PARTS) for n in range(PARTS + 1)]
    return [(a, b - a) for a, b in zip(edges, edges[1:]) if b > a]


def halo_kernel(base, extras, parity, heavy_ref, panels_ref, *refs):
    halo_ref, refs = refs[0], refs[1:]
    if extras:
        extra_ref, near, own, middle, local_sem, extra_sems, keep_sem = refs[:7]
        refs = refs[7:]
    z_sems, row_sems, corner_sems = refs
    row, col = lax.axis_index("gx"), lax.axis_index("gy")
    rows, cols = lax.axis_size("gx"), lax.axis_size("gy")
    vertical = ((lax.rem(row + 1, rows), col), (lax.rem(row + rows - 1, rows), col))
    sideways = ((row, lax.rem(col + 1, cols)), (row, lax.rem(col + cols - 1, cols)))
    barrier = pltpu.get_barrier_semaphore()
    for target in vertical + sideways:
        pl.semaphore_signal(barrier, inc=1, device_id=target, device_id_type=pl.DeviceIdType.MESH)
    pl.semaphore_wait(barrier, 4)

    def remote(src, dst, sems, target):
        return pltpu.make_async_remote_copy(
            src_ref=src,
            dst_ref=dst,
            send_sem=sems.at[0],
            recv_sem=sems.at[1],
            device_id=target,
            device_id_type=pl.DeviceIdType.MESH,
        )

    chunks = cut(0, base)
    first_tail = len(chunks)
    if extras:
        chunks += cut(base, panels_ref.shape[0])
    z_copies, others, tail_copies = [], [], []
    for n, (start, size) in enumerate(chunks):
        pair = []
        for v in range(2):
            if start < base:
                dst = halo_ref.at[6 * v + 1, pl.ds(start, size)]
            else:
                dst = near.at[v, pl.ds(start - base, size)]
            pair.append(remote(panels_ref.at[pl.ds(start, size)], dst, z_sems.at[n, v], vertical[v]))
        z_copies.append(pair)

    holds = None if parity is None else lax.rem(col, 2) == parity

    def holder(act, other=False):
        if holds is None:
            act()
        else:
            pl.when(jnp.logical_not(holds) if other else holds)(act)

    def tail_only(n, act):
        if chunks[n][0] < base:
            act()
        else:
            holder(act)

    def begin(copies):
        for copy in copies:
            copy.start()

    def arrive(copies):
        for copy in copies:
            copy.wait_recv()

    def leave(copies):
        for copy in copies:
            copy.wait_send()

    begin(z_copies[0])
    row_copies = [
        remote(panels_ref.at[pl.ds(0, base)], halo_ref.at[3 + 2 * h], row_sems.at[h], sideways[h])
        for h in range(2)
    ]
    begin(row_copies)
    others += row_copies
    for n in range(1, min(AHEAD, len(chunks))):
        tail_only(n, lambda n=n: begin(z_copies[n]))
    if extras:
        mine = pltpu.make_async_copy(panels_ref.at[pl.ds(base, own.shape[0])], own, local_sem)
        mine.start()
        mine.wait()
    for n, (start, size) in enumerate(chunks):
        tail_only(n, lambda: arrive(z_copies[n]))
        if n + AHEAD < len(chunks):
            tail_only(n + AHEAD, lambda: begin(z_copies[n + AHEAD]))
        if start < base:
            for v in range(2):
                part = pl.ds(start, size)
                copies = [
                    remote(
                        halo_ref.at[6 * v + 1, part],
                        halo_ref.at[6 * v + 2 * h, part],
                        corner_sems.at[n, v, h],
                        sideways[h],
                    )
                    for h in range(2)
                ]
                begin(copies)
                others += copies
        else:
            copies = [
                remote(
                    middle.at[e, pl.ds(start - base, size)],
                    extra_ref.at[e, 2 * h, pl.ds(start - base, size)],
                    extra_sems.at[n - first_tail, e, h],
                    sideways[h],
                )
                for e in range(extras)
                for h in range(2)
            ]

            def forward(start=start, size=size, copies=copies):
                for e in range(extras):
                    away = heavy_ref[e]
                    for p in range(start - base, start - base + size):
                        middle[e, p] = jnp.where(
                            away == 0, near[0, p], jnp.where(away == 1, own[p], near[1, p])
                        )
                begin(copies)

            holder(forward)
            tail_copies += copies
    if extras:
        kept = [
            pltpu.make_async_copy(middle.at[e], extra_ref.at[e, 1], keep_sem.at[e]) for e in range(extras)
        ]

        def keep():
            begin(kept)
            for copy in kept:
                copy.wait()

        holder(keep)
    for n in range(len(chunks)):
        tail_only(n, lambda: leave(z_copies[n]))
    for copy in others:
        copy.wait()
    if extras:
        holder(lambda: leave(tail_copies))
        holder(lambda: arrive(tail_copies), other=True)


def halo(panels, base, heavy_rows, parity):
    capacity, rows, cols = panels.shape
    extras, rest = len(heavy_rows), capacity - base
    dma = pltpu.SemaphoreType.DMA
    outs = [jax.ShapeDtypeStruct((9, base, rows, cols), panels.dtype)]
    scratch = []
    if extras:
        outs.append(jax.ShapeDtypeStruct((extras, 3, rest, rows, cols), panels.dtype))
        scratch = [
            pltpu.VMEM((2, rest, rows, cols), panels.dtype),
            pltpu.VMEM((rest, rows, cols), panels.dtype),
            pltpu.VMEM((extras, rest, rows, cols), panels.dtype),
            dma,
            dma((PARTS, extras, 2, 2)),
            dma((extras,)),
        ]
    scratch += [dma((2 * PARTS, 2, 2)), dma((2, 2)), dma((PARTS, 2, 2, 2))]
    away = jnp.stack(heavy_rows) if extras else jnp.zeros((1,), jnp.int32)
    return pl.pallas_call(
        functools.partial(halo_kernel, base, extras, parity),
        out_shape=outs,
        in_specs=[pl.BlockSpec(memory_space=pltpu.SMEM), pl.BlockSpec(memory_space=pl.ANY)],
        out_specs=[pl.BlockSpec(memory_space=pl.ANY)] * len(outs),
        scratch_shapes=scratch,
        compiler_params=pltpu.CompilerParams(
            collective_id=3 if not extras else 2 if parity is None else parity,
            has_side_effects=True,
            vmem_limit_bytes=58 * 1024 * 1024,
        ),
        name="halo_part" if extras else "halo_full",
    )(away.astype(jnp.int32), panels)


def local(counts, probes, blocks, pattern, coeffs):
    grid_rows = lax.axis_size("gx")
    grid_cols = lax.axis_size("gy")
    domains = grid_rows * grid_cols
    capacity = blocks.shape[2]
    panel_rows = blocks.shape[4]
    probe_cols = probes.shape[3] * grid_cols
    per_peer = (capacity + grid_rows - 1) // grid_rows
    my_row, my_col = lax.axis_index("gx"), lax.axis_index("gy")
    my_domain = my_row * grid_cols + my_col
    ids = jnp.arange(domains, dtype=jnp.int32)
    offsets = jnp.sum(jnp.where(ids[None, :] < ids[:, None], counts[None, :], 0), axis=1)
    my_count = jnp.sum(jnp.where(ids == my_domain, counts, 0))
    my_offset = jnp.sum(jnp.where(ids < my_domain, counts, 0))
    first_slot = (offsets + (my_row - offsets) % grid_rows) // grid_rows
    outgoing = pack(first_slot, probes[:, 0], per_peer)
    arrived = lax.all_to_all(outgoing, ("gx", "gy"), split_axis=0, concat_axis=3, tiled=True)
    arrived = arrived.reshape(per_peer, panel_rows, grid_rows, probe_cols).transpose(0, 2, 1, 3)
    arrived = jnp.concatenate([arrived, arrived], axis=1)
    start = lax.dynamic_slice_in_dim(arrived, my_offset % grid_rows, grid_rows, axis=1)
    start = start.reshape(per_peer * grid_rows, panel_rows, probe_cols)[:capacity]
    rows, table = blocks[0, 0], pattern[0, 0]

    def expand(base, heavy, parity, start):
        meta, heavy_rows = [my_count], []
        for d in heavy:
            di = (d // grid_cols - my_row + 1) % grid_rows
            dj = (d % grid_cols - my_col + 1) % grid_cols
            near = (d >= 0) & (di < 3) & (dj < 3) & (d != my_domain)
            heavy_rows.append(di)
            meta.append(jnp.where(near, di * 3 + dj, -1))
        meta = jnp.stack(meta).astype(jnp.int32)

        def run(mode, panels, *rest):
            ring, *extra = halo(panels, base, heavy_rows, parity)
            return step(mode, base, meta, table, coeffs, [panels, ring] + extra, rows, rest)

        sent, one = run(1, start)
        sent, two = run(2, sent, start)
        (out,) = run(3, sent, start, one, two)
        return out

    base = min(BASE, capacity)
    extras = max(1, domains // 32)
    over = counts > base
    rank = jnp.sum(jnp.where(ids[None, :] < ids[:, None], over[None, :], False), axis=1)
    heavy = [jnp.max(jnp.where(over & (rank == h), ids, -1)) for h in range(extras)]
    odd = sum(jnp.where((d >= 0) & (d % grid_cols % 2 == 1), 1, 0) for d in heavy)
    even = sum(jnp.where((d >= 0) & (d % grid_cols % 2 == 0), 1, 0) for d in heavy)
    branches = [
        lambda s: expand(capacity, [], None, s),
        lambda s: expand(base, heavy, None, s),
    ]
    which = jnp.where(jnp.sum(over) <= extras, 1, 0)
    if grid_cols % 2 == 0:
        branches += [lambda s: expand(base, heavy, 0, s), lambda s: expand(base, heavy, 1, s)]
        which = jnp.where(which == 0, 0, jnp.where(odd == 0, 2, jnp.where(even == 0, 3, 1)))
    if extras == 1 and grid_cols % 2 == 0:
        branches[1] = branches[0]
    out = lax.switch(which, branches, start)
    return out[None, None]


def solution(mesh):
    in_specs = (
        P(),
        P(None, "gx", None, "gy"),
        P("gx", "gy", None, None, None, None),
        P("gx", "gy", None, None),
        P(),
    )
    out_specs = P("gx", "gy", None, None, None)
    return jax.shard_map(local, mesh=mesh, in_specs=in_specs, out_specs=out_specs, check_vma=False)
```
